32 devices in a mesh: gz: 8 (over z, x), gy: 2 (over core), gx: 2 (over y).
Axes of the slice: x: 2, y: 2, z: 4, core: 2. Of those that a mesh axis runs over, the one named last changes fastest.
Arguments:
- grid_input: bfloat16 [64, 32, 4096], P('gz', 'gy', 'gx'), may hold values from -6 to 6
- pre_one: bfloat16 [64, 32, 4096], P('gz', 'gy', 'gx'), may hold values from -5.875 to 4.125
- pre_two: bfloat16 [64, 32, 4096], P('gz', 'gy', 'gx'), may hold values from -8 to 8
- grad_output: bfloat16 [64, 32, 4096], P('gz', 'gy', 'gx'), may hold values from -6 to 6
- spectral_one: bfloat16 [16, 16, 16, 4096], P('gz', 'gy', 'gx'), may hold values from -1.5 to 1.5
- spectral_two: bfloat16 [16, 16, 16, 4096], P('gz', 'gy', 'gx'), may hold values from -1.5 to 1.5
- point_one: bfloat16 [64, 64], replicated, may hold values from -0.75 to 0.75
- point_two: bfloat16 [64, 64], replicated, may hold values from -0.75 to 0.75
Outputs:
- input_grad: bfloat16 [64, 32, 4096], P('gz', 'gy', 'gx')
- spectral_grad_one: float32 [16, 16, 16, 4096], P('gz', 'gy', 'gx')
- spectral_grad_two: float32 [16, 16, 16, 4096], P('gz', 'gy', 'gx')
- point_grad_one: float32 [64, 64], replicated
- point_grad_two: float32 [64, 64], replicated
The draws below stay inside these ranges and needn't reach their ends.
All inputs are finite; a program needn't handle non-finite values.
Results may differ from the reference program's by a relative error of at most 0.012.
Values sent between devices are 32-bit elements; how exact they have to be, the bound alone decides.
A program may use at most 64 MiB of HBM per device.

```python
import math
import jax
import jax.numpy as jnp
from jax import lax

C = 64
MX = 16
MY = 16
MZ = 16
CX = 8
CY = 16
CZ = 32
NX = 64
NY = 32
NZ = 64


def draw_pre_one(key, part):
    values = jax.random.normal(key, (NX, NY, NZ * C), jnp.float32)
    return (jnp.clip(values, -5.0, 5.0) - 0.875).astype(jnp.bfloat16)


def block_levels(rng, shape, pieces, least, top_value):
    def one(dim, shards_of):
        heights = jax.random.uniform(jax.random.fold_in(jax.random.fold_in(rng, 6), dim), (shards_of,), jnp.float32, least / len(pieces), top_value / len(pieces))
        return jnp.repeat(jnp.exp(heights), shape[dim] // shards_of).reshape((-1,) + (1,) * (len(shape) - dim - 1))

    gain = one(*pieces[0])
    for cut in pieces[1:]:
        gain = gain * one(*cut)
    return gain


def noise(key, shape, width, limit, cuts=(), kind=jnp.bfloat16):
    loudness = block_levels(key, shape, cuts, -0.22, 0.18) if cuts else 1.0
    values = jax.random.normal(key, shape, jnp.float32) * width * loudness
    return jnp.minimum(jnp.maximum(values, -limit), limit).astype(kind)


def setup_inputs(seed: int = 0) -> dict:
    streams_of = jax.random.split(jax.random.key(seed), 9)
    return {
        "grid_input": noise(streams_of[0], (NX, NY, NZ * C), 1.0, 6.0, ((0, 8), (1, 2), (2, 2))),
        "pre_one": draw_pre_one(jax.random.fold_in(streams_of[8], 71), 0),
        "pre_two": noise(streams_of[2], (NX, NY, NZ * C), 1.5, 8.0, ((0, 8), (1, 2), (2, 2))),
        "grad_output": noise(streams_of[3], (NX, NY, NZ * C), 1.0, 6.0, ((0, 8), (1, 2), (2, 2))),
        "spectral_one": noise(streams_of[4], (MX, MY, MZ, C * C), (C // 4) ** -0.5, 1.5, ((0, 8), (1, 2), (2, 2))),
        "spectral_two": noise(streams_of[5], (MX, MY, MZ, C * C), (C // 4) ** -0.5, 1.5, ((0, 8), (1, 2), (2, 2))),
        "point_one": noise(streams_of[6], (C, C), C ** -0.5, 0.75),
        "point_two": noise(streams_of[7], (C, C), C ** -0.5, 0.75),
    }


highest = lax.Precision.HIGHEST
inv_root_two = 0.7071067811865476
inv_root_tau = 0.3989422804014327


def frequency_list(mode_count, length):
    position = jnp.arange(mode_count, dtype=jnp.int32)
    return jnp.where(position < mode_count // 2, position, length - mode_count + position).astype(jnp.int32)


def cell_positions(cell_count, device_count):
    rows = jnp.arange(cell_count * device_count, dtype=jnp.int32)
    return ((rows % cell_count) * device_count + rows // cell_count).astype(jnp.int32)


def cas_table(mode_count, length, positions):
    frequency = frequency_list(mode_count, length)
    product = (frequency[:, None] * positions[None, :]) % length
    phase = product.astype(jnp.float32) * (2.0 * math.pi / length)
    return (jnp.cos(phase) + jnp.sin(phase)).astype(jnp.bfloat16)


def gelu_value(pre_value):
    return pre_value * 0.5 * (1.0 + jax.scipy.special.erf(pre_value * inv_root_two))


def gelu_slope(pre_value):
    normal_cdf = 0.5 * (1.0 + jax.scipy.special.erf(pre_value * inv_root_two))
    return normal_cdf + pre_value * jnp.exp(-0.5 * pre_value * pre_value) * inv_root_tau


def analyse(values, tables):
    table_x, table_y, table_z = [t.astype(jnp.float32) for t in tables]
    along_z = jnp.einsum('xyzc,kz->xykc', values.astype(jnp.float32), table_z, precision=highest)
    along_y = jnp.einsum('xykc,jy->xjkc', along_z, table_y, precision=highest)
    return jnp.einsum('xjkc,ix->ijkc', along_y, table_x, precision=highest)


def synthesise(spectra, tables):
    table_x, table_y, table_z = [t.astype(jnp.float32) for t in tables]
    along_z = jnp.einsum('ijkc,kz->ijzc', spectra, table_z, precision=highest)
    along_y = jnp.einsum('ijzc,jy->iyzc', along_z, table_y, precision=highest)
    return jnp.einsum('iyzc,ix->xyzc', along_y, table_x, precision=highest)


def layer_back(layer_in, pre_act, upstream, spectral, point, tables, scales):
    analysis, synthesis, cell_scale = scales
    channels = point.shape[0]
    pre_grad = (upstream * gelu_slope(pre_act.astype(jnp.float32))).astype(jnp.bfloat16)
    hat_in = analysis * analyse(layer_in, tables)
    hat_grad = synthesis * analyse(pre_grad, tables)
    weights = spectral.astype(jnp.float32).reshape(hat_in.shape + (channels,))
    spec_grad = (hat_in[..., :, None] * hat_grad[..., None, :]).reshape(spectral.shape)
    hat_back = jnp.einsum('ijkao,ijko->ijka', weights, hat_grad, precision=highest)
    flat_in = layer_in.reshape(-1, channels)
    flat_grad = pre_grad.reshape(-1, channels)
    point_grad = cell_scale * jnp.dot(flat_in.T, flat_grad, preferred_element_type=jnp.float32)
    local_term = jnp.dot(flat_grad, point.T, preferred_element_type=jnp.float32).reshape(layer_in.shape)
    down = analysis * synthesise(hat_back, tables) + local_term
    return down, spec_grad, point_grad


def reference(grid_input, pre_one, pre_two, grad_output, spectral_one, spectral_two, point_one, point_two):
    shape_four = (NX, NY, NZ, C)
    tables = (cas_table(MX, NX, cell_positions(CX, NX // CX)),
              cas_table(MY, NY, cell_positions(CY, NY // CY)),
              cas_table(MZ, NZ, cell_positions(CZ, NZ // CZ)))
    total_cells = NX * NY * NZ
    total_modes = MX * MY * MZ
    scales = ((total_cells * total_modes) ** -0.25, total_cells ** -0.5, total_cells ** -0.5)
    first_in = grid_input.reshape(shape_four)
    first_pre = pre_one.reshape(shape_four)
    second_pre = pre_two.reshape(shape_four)
    upstream = grad_output.reshape(shape_four).astype(jnp.float32)
    middle = gelu_value(first_pre.astype(jnp.float32)).astype(jnp.bfloat16)
    down_two, spec_two, grad_two = layer_back(middle, second_pre, upstream, spectral_two, point_two, tables, scales)
    down_one, spec_one, grad_one = layer_back(first_in, first_pre, down_two, spectral_one, point_one, tables, scales)
    input_grad = down_one.astype(jnp.bfloat16).reshape(NX, NY, NZ * C)
    return (input_grad, spec_one, spec_two, grad_one, grad_two)
```

```python
import functools
import math

import jax
import jax.numpy as jnp
import ml_dtypes
import numpy as np
from jax import lax
from jax.experimental import pallas as pl
from jax.experimental.pallas import tpu as pltpu
from jax.sharding import PartitionSpec as P

MX = 16
MY = 16
MZ = 16

inv_root_two = 0.7071067811865476
inv_root_tau = 0.3989422804014327
bf16 = jnp.bfloat16
f32 = jnp.float32


def cas_tables(mode_count, cells, devices):
    length = cells * devices
    mode = np.arange(mode_count)
    frequency = np.where(mode < mode_count // 2, mode, length - mode_count + mode)
    position = np.arange(cells)[None, :] * devices + np.arange(devices)[:, None]
    product = (frequency[None, :, None] * position[:, None, :]) % length
    phase = product.astype(np.float32) * np.float32(2.0 * math.pi / length)
    return (np.cos(phase) + np.sin(phase)).astype(ml_dtypes.bfloat16).astype(np.float32)


def const(values):
    return jnp.asarray(np.asarray(values).astype(ml_dtypes.bfloat16))


def gelu_both(pre_value):
    cdf = 0.5 * (1.0 + lax.erf(pre_value * inv_root_two))
    slope = cdf + pre_value * jnp.exp(-0.5 * pre_value * pre_value) * inv_root_tau
    return pre_value * cdf, slope


def mm(a, b):
    return jnp.dot(a.astype(bf16), b.astype(bf16), preferred_element_type=f32)


def mm_t(a, b):
    return lax.dot_general(
        a.astype(bf16), b.astype(bf16), (((1,), (1,)), ((), ())), preferred_element_type=f32
    )


def tmm(a, b):
    return lax.dot_general(
        a.astype(bf16), b.astype(bf16), (((0,), (0,)), ((), ())), preferred_element_type=f32
    )


def layer_kernel(cfg, *refs):
    nz, ny, nx = cfg["nz"], cfg["ny"], cfg["nx"]
    first = cfg["first"]
    brow, blane = cfg["brow"], cfg["blane"]
    mrow = cfg["mrow"]
    a_scale, b_scale = cfg["scales"]
    chan = cfg["chan"]
    n_a = ny * nx
    names = cfg["names"]
    r = dict(zip(names, refs))
    kz, ay, ax, axt, ayt = r["kz"], r["ay"], r["ax"], r["axt"], r["ayt"]
    gz, gy, gx = lax.axis_index("gz"), lax.axis_index("gy"), lax.axis_index("gx")

    def wrap(v, n):
        return lax.rem(v, n)

    def a_peer(j):
        return wrap(gy + j // nx, ny), wrap(gx + j % nx, nx)

    def a_device(j):
        py, px = a_peer(j)
        return (gz, py, px)

    def b_device(j):
        return (wrap(gz + j, nz), gy, gx)

    barrier = pltpu.get_barrier_semaphore()
    for j in range(1, n_a):
        pl.semaphore_signal(barrier, 1, device_id=a_device(j), device_id_type=pl.DeviceIdType.MESH)
    for j in range(1, nz):
        pl.semaphore_signal(barrier, 1, device_id=b_device(j), device_id_type=pl.DeviceIdType.MESH)

    width = kz.shape[1]
    tile = 256
    lanes = kz.shape[0]
    copies = []

    def remote(src, dst, sem, j, dev):
        c = pltpu.make_async_remote_copy(
            src_ref=src, dst_ref=dst, send_sem=r[sem + "_s"].at[j], recv_sem=r[sem + "_r"].at[j],
            device_id=dev, device_id_type=pl.DeviceIdType.MESH,
        )
        c.start()
        copies.append(c)
        return c

    def analyse(src, t):
        table_y = ay[gy]

        def body(n, carry):
            cols = pl.ds(pl.multiple_of(n * tile, tile), tile)
            part = mm(src[...], kz[:, cols])
            r["y"][t, :, cols] = mm(table_y, part)
            return carry

        lax.fori_loop(0, width // tile, body, 0)

    def block(py, px):
        return (
            pl.ds(pl.multiple_of(py * brow, brow), brow),
            pl.ds(pl.multiple_of(px * blane, blane), blane),
        )

    def start_a(t):
        out = []
        for j in range(1, n_a):
            rows, cols = block(*a_peer(j))
            out.append(
                remote(r["y"].at[t, rows, cols], r["land_a"].at[t, j], "a%d" % t, j, a_device(j))
            )
        return out

    def finish_a(t, cs):
        rows, cols = block(gy, gx)
        for c in cs:
            c.wait_recv()
        total = r["y"][t, rows, cols]
        for j in range(1, n_a):
            total = total + r["land_a"][t, j]
        part = mm(ax[gz], total)
        for s in range(nz):
            r["p"][t, s] = part[s * mrow : (s + 1) * mrow, :]
        out = []
        for j in range(1, nz):
            dev = b_device(j)
            out.append(remote(r["p"].at[t, dev[0]], r["land_b"].at[t, j], "b%d" % t, j, dev))
        return out

    def finish_b(t, cs, scale):
        for c in cs:
            c.wait_recv()
        total = r["p"][t, gz]
        for j in range(1, nz):
            total = total + r["land_b"][t, j]
        spread = mm(r["rep"][...], total * scale) * r["mask"][...]
        return mm(spread, r["fold"][...])

    analyse(r["dz"], 0)
    pl.semaphore_wait(barrier, n_a + nz - 2)
    wait_a = start_a(0)
    if first:
        lane = lax.broadcasted_iota(jnp.int32, (chan, 2 * chan), 1)

        def point_part(left, right):
            total = jnp.zeros((2 * chan, 2 * chan), f32)

            def body(n, acc):
                cols = pl.ds(pl.multiple_of(n * 2 * chan, 2 * chan), 2 * chan)
                return acc + tmm(left[:, cols], right[:, cols])

            return lax.fori_loop(0, lanes // (2 * chan), body, total)

        pa = point_part(r["mid"], r["dz_two"])
        pb = point_part(r["gin"], r["dz"])
        low = lane < chan
        keep = jnp.where(low, pa[:chan], pb[chan:])
        turn = jnp.where(low, pb[:chan], pa[chan:])
        r["pt_a"][gy * nx + gx] = keep + pltpu.roll(turn, chan, 1)
        wait_pa = [
            remote(
                r["pt_a"].at[gy * nx + gx], r["pt_a"].at[gy * nx + gx], "pa", j, a_device(j)
            )
            for j in range(1, n_a)
        ]
    else:
        analyse(r["mid"], 1)
        wait_a1 = start_a(1)
        analyse(r["gin"], 2)
        wait_a2 = start_a(2)
    wait_b = finish_a(0, wait_a)
    tall = mm_t(r["eye"][...], r["point"][...])
    square = mm_t(tall, r["eye"][...])
    row_i = lax.broadcasted_iota(jnp.int32, square.shape, 0) // chan
    col_i = lax.broadcasted_iota(jnp.int32, square.shape, 1) // chan
    r["p4"][...] = jnp.where(row_i == col_i, square, 0.0).astype(bf16)
    if first:
        for c in wait_pa:
            c.wait_recv()
        total = r["pt_a"][0]
        for j in range(1, n_a):
            total = total + r["pt_a"][j]
        r["pt_b"][gz] = total
        wait_pb = [
            remote(r["pt_b"].at[gz], r["pt_b"].at[gz], "pb", j, b_device(j))
            for j in range(1, nz)
        ]
    hat = finish_b(0, wait_b, b_scale)
    wide = r["weights"].shape[1]
    prod_tile = jnp.concatenate([hat] * (512 // hat.shape[1]), axis=1)
    back = jnp.zeros((hat.shape[0], chan), f32)
    for n in range(wide // 512):
        w = r["weights"][:, n * 512 : (n + 1) * 512].astype(f32)
        back = back + mm(w * prod_tile, r["sum_o"][n * 512 : (n + 1) * 512, :])
    spread = mm(back, r["spread"][...]) * r["mask"][...]
    r["c"][gz] = tmm(r["rep"][...], spread)
    wait_c = [
        remote(r["c"].at[gz], r["c"].at[gz], "c", j, b_device(j)) for j in range(1, nz)
    ]
    if not first:
        wait_b1 = finish_a(1, wait_a1)
        wait_b2 = finish_a(2, wait_a2)
    for c in wait_c:
        c.wait_recv()
    for s in range(nz):
        r["cat"][s * mrow : (s + 1) * mrow, :] = r["c"][s]
    rows, cols = block(gy, gx)
    r["v"][rows, cols] = mm(axt[gz], r["cat"][...])
    wait_d = [
        remote(r["v"].at[rows, cols], r["v"].at[rows, cols], "d", j, a_device(j))
        for j in range(1, n_a)
    ]
    if first:
        hat_in = r["hat_in"][...]
    else:
        hat_in = finish_b(1, wait_b1, a_scale)
        r["hat_out"][...] = finish_b(2, wait_b2, a_scale)
    low_in = hat_in[:, :chan]
    for n in range(wide // 512):
        cs = slice(n * 512, (n + 1) * 512)
        r["spec"][:, cs] = mm_t(low_in, r["sum_o"][cs, :]) * prod_tile
    if first:
        for c in wait_pb:
            c.wait_recv()
        total = r["pt_b"][0]
        for j in range(1, nz):
            total = total + r["pt_b"][j]
        r["pt"][...] = total * b_scale
    for c in wait_d:
        c.wait_recv()
    r["v2"][...] = (mm(ayt[gy], r["v"][...]) * a_scale).astype(bf16)

    def body(n, carry):
        cs = pl.ds(pl.multiple_of(n * tile, tile), tile)
        r["down"][:, cs] = (
            mm_t(r["v2"][...], kz[cs, :]) + mm(r["dz"][:, cs], r["p4"][...])
        ).astype(r["down"].dtype)
        return carry

    lax.fori_loop(0, lanes // tile, body, 0)
    for c in copies:
        c.wait_send()


def on_device(
    grid_input, pre_one, pre_two, grad_output, spectral_one, spectral_two, point_one, point_two
):
    chan = point_one.shape[0]
    nz, ny, nx = (lax.axis_size("gz"), lax.axis_size("gy"), lax.axis_size("gx"))
    cx, cy = grid_input.shape[:2]
    lanes = grid_input.shape[2]
    cz = lanes // chan
    qx, qy, qz = MX // nz, MY // ny, MZ // nx
    total_cells = cx * nz * cy * ny * cz * nx
    b_scale = total_cells ** (-0.5)
    a_scale = (total_cells * MX * MY * MZ) ** (-0.25)
    tx, ty, tz = cas_tables(MX, cx, nz), cas_tables(MY, cy, ny), cas_tables(MZ, cz, nx)
    eye = np.eye(chan, dtype=np.float32)
    kz_all = np.zeros((nx, cz, chan, MZ, chan), ml_dtypes.bfloat16)
    diag = np.arange(chan)
    kz_all[:, :, diag, :, diag] = tz.transpose(0, 2, 1).astype(ml_dtypes.bfloat16)[None]
    kz = lax.dynamic_index_in_dim(
        const(kz_all.reshape(nx, lanes, MZ * chan)), lax.axis_index("gx"), 0, False
    )
    ay = np.einsum("dky,xw->dkxwy", ty, np.eye(cx)).reshape(ny, MY * cx, cx * cy)
    ax = np.einsum("dkx,ab->dkabx", tx, np.eye(qy)).reshape(nz, MX * qy, qy * cx)
    modes = qx * qy * qz
    mrow = qx * qy
    blane = qz * chan
    mode = np.arange(modes)
    rep = (mode[:, None] // qz == np.arange(mrow)[None, :]).astype(np.float32)
    mask = (mode[:, None] % qz == np.arange(blane)[None, :] // chan).astype(np.float32)
    fold = np.tile(np.concatenate([eye, eye], axis=1), (qz, 1))
    spread = np.tile(eye, (1, qz))
    sum_o = np.repeat(eye, chan, axis=0)
    eye4 = np.tile(eye, (256 // chan, 1))
    tables = {
        "kz": kz,
        "ay": const(ay),
        "ax": const(ax),
        "axt": const(ax.transpose(0, 2, 1)),
        "ayt": const(ay.transpose(0, 2, 1)),
        "rep": const(rep),
        "mask": jnp.asarray(mask),
        "fold": const(fold),
        "spread": const(spread),
        "sum_o": const(sum_o),
        "eye": const(eye4),
    }
    rows = cx * cy
    brow = qy * cx
    n_a = ny * nx

    def call(first, ins):
        args = dict(ins, **tables)
        t = 1 if first else 3
        outs = {
            "down": jax.ShapeDtypeStruct((rows, lanes), bf16 if first else f32),
            "spec": jax.ShapeDtypeStruct((modes, chan * chan), f32),
        }
        if first:
            outs["pt"] = jax.ShapeDtypeStruct((chan, 2 * chan), f32)
        else:
            outs["hat_out"] = jax.ShapeDtypeStruct((modes, 2 * chan), f32)
        scratch = {
            "y": pltpu.VMEM((t, MY * cx, MZ * chan), f32),
            "land_a": pltpu.VMEM((t, n_a, brow, blane), f32),
            "p": pltpu.VMEM((t, nz, mrow, blane), f32),
            "land_b": pltpu.VMEM((t, nz, mrow, blane), f32),
            "c": pltpu.VMEM((nz, mrow, blane), f32),
            "cat": pltpu.VMEM((nz * mrow, blane), f32),
            "v": pltpu.VMEM((MY * cx, MZ * chan), f32),
            "v2": pltpu.VMEM((rows, MZ * chan), bf16),
            "p4": pltpu.VMEM((256, 256), bf16),
        }
        sems = {"c": nz, "d": n_a}
        for k in range(t):
            sems["a%d" % k] = n_a
            sems["b%d" % k] = nz
        if first:
            scratch["pt_a"] = pltpu.VMEM((n_a, chan, 2 * chan), f32)
            scratch["pt_b"] = pltpu.VMEM((nz, chan, 2 * chan), f32)
            sems["pa"] = n_a
            sems["pb"] = nz
        for k, n in sems.items():
            scratch[k + "_s"] = pltpu.SemaphoreType.DMA((n,))
            scratch[k + "_r"] = pltpu.SemaphoreType.DMA((n,))
        cfg = dict(
            nz=nz, ny=ny, nx=nx, first=first, brow=brow, blane=blane, mrow=mrow,
            scales=(a_scale, b_scale), chan=chan,
            names=list(args) + list(outs) + list(scratch),
        )
        vmem = pl.BlockSpec(memory_space=pltpu.VMEM)
        got = pl.pallas_call(
            functools.partial(layer_kernel, cfg),
            out_shape=list(outs.values()),
            in_specs=[vmem] * len(args),
            out_specs=[vmem] * len(outs),
            scratch_shapes=list(scratch.values()),
            compiler_params=pltpu.CompilerParams(
                collective_id=1 if first else 0,
                has_side_effects=True,
                vmem_limit_bytes=48 * 1024 * 1024,
            ),
            name="layer_one" if first else "layer_two",
        )(*args.values())
        return dict(zip(outs, got))

    flat = (rows, lanes)
    gin = grid_input.reshape(flat)
    value_one, slope_one = gelu_both(pre_one.reshape(flat).astype(f32))
    _, slope_two = gelu_both(pre_two.reshape(flat).astype(f32))
    mid = value_one.astype(bf16)
    dz_two = (grad_output.reshape(flat).astype(f32) * slope_two).astype(bf16)
    two = call(
        False,
        {
            "dz": dz_two,
            "mid": mid,
            "gin": gin,
            "weights": spectral_two.reshape(modes, chan * chan),
            "point": point_two,
        },
    )
    dz_one = (two["down"] * slope_one).astype(bf16)
    one = call(
        True,
        {
            "dz": dz_one,
            "mid": mid,
            "gin": gin,
            "dz_two": dz_two,
            "hat_in": two["hat_out"],
            "weights": spectral_one.reshape(modes, chan * chan),
            "point": point_one,
        },
    )
    return (
        one["down"].reshape(grid_input.shape),
        one["spec"].reshape(spectral_one.shape),
        two["spec"].reshape(spectral_two.shape),
        one["pt"][:, chan:],
        one["pt"][:, :chan],
    )


def solution(mesh):
    grid = P("gz", "gy", "gx")
    spec = P("gz", "gy", "gx", None)
    return jax.shard_map(
        on_device,
        mesh=mesh,
        in_specs=(grid, grid, grid, grid, spec, spec, P(), P()),
        out_specs=(grid, spec, spec, P(), P()),
        check_vma=False,
    )
```

```python
import functools
import math

import jax
import jax.numpy as jnp
import ml_dtypes
import numpy as np
from jax import lax
from jax.experimental import pallas as pl
from jax.experimental.pallas import tpu as pltpu
from jax.sharding import PartitionSpec as P

MX = 16
MY = 16
MZ = 16

inv_root_two = 0.7071067811865476
inv_root_tau = 0.3989422804014327
bf16 = jnp.bfloat16
f32 = jnp.float32


def cas_tables(mode_count, cells, devices):
    length = cells * devices
    mode = np.arange(mode_count)
    frequency = np.where(mode < mode_count // 2, mode, length - mode_count + mode)
    position = np.arange(cells)[None, :] * devices + np.arange(devices)[:, None]
    product = (frequency[None, :, None] * position[:, None, :]) % length
    phase = product.astype(np.float32) * np.float32(2.0 * math.pi / length)
    return (np.cos(phase) + np.sin(phase)).astype(ml_dtypes.bfloat16).astype(np.float32)


def const(values):
    return jnp.asarray(np.asarray(values).astype(ml_dtypes.bfloat16))


def gelu_both(pre_value):
    cdf = 0.5 * (1.0 + lax.erf(pre_value * inv_root_two))
    slope = cdf + pre_value * jnp.exp(-0.5 * pre_value * pre_value) * inv_root_tau
    return pre_value * cdf, slope


def mm(a, b):
    return jnp.dot(a.astype(bf16), b.astype(bf16), preferred_element_type=f32)


def mm_t(a, b):
    return lax.dot_general(
        a.astype(bf16), b.astype(bf16), (((1,), (1,)), ((), ())), preferred_element_type=f32
    )


def tmm(a, b):
    return lax.dot_general(
        a.astype(bf16), b.astype(bf16), (((0,), (0,)), ((), ())), preferred_element_type=f32
    )


def layer_kernel(cfg, *refs):
    nz, ny, nx = cfg["nz"], cfg["ny"], cfg["nx"]
    first = cfg["first"]
    brow, blane = cfg["brow"], cfg["blane"]
    mrow = cfg["mrow"]
    a_scale, b_scale = cfg["scales"]
    chan = cfg["chan"]
    n_a = ny * nx
    names = cfg["names"]
    r = dict(zip(names, refs))
    kz, ay, ax, axt, ayt = r["kz"], r["ay"], r["ax"], r["axt"], r["ayt"]
    half = blane // 2
    gz, gy, gx = lax.axis_index("gz"), lax.axis_index("gy"), lax.axis_index("gx")

    def wrap(v, n):
        return lax.rem(v, n)

    def a_peer(j):
        return wrap(gy + j // nx, ny), wrap(gx + j % nx, nx)

    def a_device(j):
        py, px = a_peer(j)
        return (gz, py, px)

    def b_device(j):
        return (wrap(gz + j, nz), gy, gx)

    width = kz.shape[1]
    tile = 256
    lanes = kz.shape[0]
    loads = {}
    for h in range(2):
        for px in range(nx):
            n = 2 * px + h
            cols = slice(n * half, (n + 1) * half)
            loads[n] = pltpu.make_async_copy(
                r["kz_all"].at[gx, :, cols], kz.at[:, cols], r["kz_sem"].at[n]
            )
            loads[n].start()

    barrier = pltpu.get_barrier_semaphore()
    for j in range(1, n_a):
        pl.semaphore_signal(barrier, 1, device_id=a_device(j), device_id_type=pl.DeviceIdType.MESH)
    for j in range(1, nz):
        pl.semaphore_signal(barrier, 1, device_id=b_device(j), device_id_type=pl.DeviceIdType.MESH)

    copies = []

    def remote(src, dst, sem, j, dev, h=0):
        c = pltpu.make_async_remote_copy(
            src_ref=src, dst_ref=dst,
            send_sem=r[sem + "_s"].at[h, j], recv_sem=r[sem + "_r"].at[h, j],
            device_id=dev, device_id_type=pl.DeviceIdType.MESH,
        )
        c.start()
        copies.append(c)
        return c

    def analyse(src, t):
        table_y = ay[gy]

        def body(n, carry):
            cols = pl.ds(pl.multiple_of(n * tile, tile), tile)
            part = mm(src[...], kz[:, cols])
            r["y"][t, :, cols] = mm(table_y, part)
            return carry

        lax.fori_loop(0, width // tile, body, 0)

    def block(py, px, h=None):
        size = blane if h is None else half
        return (
            pl.ds(pl.multiple_of(py * brow, brow), brow),
            pl.ds(pl.multiple_of(px * blane + (h or 0) * half, half), size),
        )

    a_order = sorted(range(1, n_a), key=lambda j: (j % nx == 0, j))

    def start_a(t, h):
        out = []
        for j in a_order:
            rows, cols = block(*a_peer(j), h)
            out.append(
                remote(
                    r["y"].at[t, rows, cols], r["land_a"].at[t, h, j], "a%d" % t, j, a_device(j), h
                )
            )
        return out

    def finish_a(t, cs):
        out = []
        for h in range(2):
            rows, cols = block(gy, gx, h)
            for c in cs[h]:
                c.wait_recv()
            total = r["y"][t, rows, cols]
            for j in range(1, n_a):
                total = total + r["land_a"][t, h, j]
            part = mm(ax[gz], total)
            for s in range(nz):
                r["p"][t, h, s] = part[s * mrow : (s + 1) * mrow, :]
            for j in range(1, nz):
                dev = b_device(j)
                out.append(
                    remote(r["p"].at[t, h, dev[0]], r["land_b"].at[t, h, j], "b%d" % t, j, dev, h)
                )
        return out

    def finish_b(t, cs, scale):
        for c in cs:
            c.wait_recv()
        parts = []
        for h in range(2):
            total = r["p"][t, h, gz]
            for j in range(1, nz):
                total = total + r["land_b"][t, h, j]
            parts.append(total)
        total = jnp.concatenate(parts, axis=1)
        spread = mm(r["rep"][...], total * scale) * r["mask"][...]
        return mm(spread, r["fold"][...])

    wait_a = []
    for h in range(2):
        for px in range(nx):
            n = 2 * px + h
            cols = slice(n * half, (n + 1) * half)
            loads[n].wait()
            r["y"][0, :, cols] = mm(ay[gy], mm(r["dz"][...], kz[:, cols]))
        if h == 0:
            pl.semaphore_wait(barrier, n_a + nz - 2)
        wait_a.append(start_a(0, h))
    if first:
        lane = lax.broadcasted_iota(jnp.int32, (chan, 2 * chan), 1)

        def point_part(left, right):
            total = jnp.zeros((2 * chan, 2 * chan), f32)

            def body(n, acc):
                cols = pl.ds(pl.multiple_of(n * 2 * chan, 2 * chan), 2 * chan)
                return acc + tmm(left[:, cols], right[:, cols])

            return lax.fori_loop(0, lanes // (2 * chan), body, total)

        pa = point_part(r["mid"], r["dz_two"])
        pb = point_part(r["gin"], r["dz"])
        low = lane < chan
        keep = jnp.where(low, pa[:chan], pb[chan:])
        turn = jnp.where(low, pb[:chan], pa[chan:])
        r["pt_a"][gy * nx + gx] = keep + pltpu.roll(turn, chan, 1)
        wait_pa = [
            remote(
                r["pt_a"].at[gy * nx + gx], r["pt_a"].at[gy * nx + gx], "pa", j, a_device(j)
            )
            for j in range(1, n_a)
        ]
    else:
        analyse(r["mid"], 1)
        wait_a1 = [start_a(1, 0), start_a(1, 1)]
        analyse(r["gin"], 2)
        wait_a2 = [start_a(2, 0), start_a(2, 1)]
    wait_b = finish_a(0, wait_a)
    tall = mm_t(r["eye"][...], r["point"][...])
    square = mm_t(tall, r["eye"][...])
    row_i = lax.broadcasted_iota(jnp.int32, square.shape, 0) // chan
    col_i = lax.broadcasted_iota(jnp.int32, square.shape, 1) // chan
    r["p4"][...] = jnp.where(row_i == col_i, square, 0.0).astype(bf16)
    if first:
        for c in wait_pa:
            c.wait_recv()
        total = r["pt_a"][0]
        for j in range(1, n_a):
            total = total + r["pt_a"][j]
        r["pt_b"][gz] = total
        wait_pb = [
            remote(r["pt_b"].at[gz], r["pt_b"].at[gz], "pb", j, b_device(j))
            for j in range(1, nz)
        ]
    hat = finish_b(0, wait_b, b_scale)
    wide = r["weights"].shape[1]
    prod_tile = jnp.concatenate([hat] * (512 // hat.shape[1]), axis=1)
    back = jnp.zeros((hat.shape[0], chan), f32)
    for n in range(wide // 512):
        w = r["weights"][:, n * 512 : (n + 1) * 512].astype(f32)
        back = back + mm(w * prod_tile, r["sum_o"][n * 512 : (n + 1) * 512, :])
    spread = mm(back, r["spread"][...]) * r["mask"][...]
    mixed = tmm(r["rep"][...], spread)
    wait_c = []
    for h in range(2):
        r["c"][h, gz] = mixed[:, h * half : (h + 1) * half]
        wait_c.append(
            [
                remote(r["c"].at[h, gz], r["c"].at[h, gz], "c", j, b_device(j), h)
                for j in range(1, nz)
            ]
        )
    if not first:
        wait_b1 = finish_a(1, wait_a1)
        wait_b2 = finish_a(2, wait_a2)
    wait_d = []
    for h in range(2):
        for c in wait_c[h]:
            c.wait_recv()
        for s in range(nz):
            r["cat"][s * mrow : (s + 1) * mrow, :] = r["c"][h, s]
        rows, cols = block(gy, gx, h)
        r["v"][rows, cols] = mm(axt[gz], r["cat"][...])
        wait_d += [
            remote(r["v"].at[rows, cols], r["v"].at[rows, cols], "d", j, a_device(j), h)
            for j in a_order
        ]
    r["hat"][...] = hat
    if not first:
        r["hat_in_two"][...] = finish_b(1, wait_b1, a_scale)
        r["hat_in_one"][...] = finish_b(2, wait_b2, a_scale)
    if first:
        for c in wait_pb:
            c.wait_recv()
        total = r["pt_b"][0]
        for j in range(1, nz):
            total = total + r["pt_b"][j]
        r["pt"][...] = total * b_scale
    for c in wait_d:
        c.wait_recv()
    r["v2"][...] = (mm(ayt[gy], r["v"][...]) * a_scale).astype(bf16)

    def body(n, carry):
        cs = pl.ds(pl.multiple_of(n * tile, tile), tile)
        r["down"][:, cs] = (
            mm_t(r["v2"][...], kz[cs, :]) + mm(r["dz"][:, cs], r["p4"][...])
        ).astype(r["down"].dtype)
        return carry

    lax.fori_loop(0, lanes // tile, body, 0)
    for c in copies:
        c.wait_send()


def outer_kernel(chan, in_one, dz_one, in_two, dz_two, sum_o, spec_one, spec_two):
    for hat_in, hat, out in ((in_one, dz_one, spec_one), (in_two, dz_two, spec_two)):
        times = out.shape[1] // hat.shape[1]
        out[...] = mm_t(hat_in[:, :chan], sum_o[...]) * jnp.concatenate([hat[...]] * times, axis=1)


def on_device(
    grid_input, pre_one, pre_two, grad_output, spectral_one, spectral_two, point_one, point_two
):
    chan = point_one.shape[0]
    nz, ny, nx = (lax.axis_size("gz"), lax.axis_size("gy"), lax.axis_size("gx"))
    cx, cy = grid_input.shape[:2]
    lanes = grid_input.shape[2]
    cz = lanes // chan
    qx, qy, qz = MX // nz, MY // ny, MZ // nx
    total_cells = cx * nz * cy * ny * cz * nx
    b_scale = total_cells ** (-0.5)
    a_scale = (total_cells * MX * MY * MZ) ** (-0.25)
    tx, ty, tz = cas_tables(MX, cx, nz), cas_tables(MY, cy, ny), cas_tables(MZ, cz, nx)
    eye = np.eye(chan, dtype=np.float32)
    kz_all = np.zeros((nx, cz, chan, MZ, chan), ml_dtypes.bfloat16)
    diag = np.arange(chan)
    kz_all[:, :, diag, :, diag] = tz.transpose(0, 2, 1).astype(ml_dtypes.bfloat16)[None]
    kz_all = const(kz_all.reshape(nx, lanes, MZ * chan))
    ay = np.einsum("dky,xw->dkxwy", ty, np.eye(cx)).reshape(ny, MY * cx, cx * cy)
    ax = np.einsum("dkx,ab->dkabx", tx, np.eye(qy)).reshape(nz, MX * qy, qy * cx)
    modes = qx * qy * qz
    mrow = qx * qy
    blane = qz * chan
    mode = np.arange(modes)
    rep = (mode[:, None] // qz == np.arange(mrow)[None, :]).astype(np.float32)
    mask = (mode[:, None] % qz == np.arange(blane)[None, :] // chan).astype(np.float32)
    fold = np.tile(np.concatenate([eye, eye], axis=1), (qz, 1))
    spread = np.tile(eye, (1, qz))
    sum_o = np.repeat(eye, chan, axis=0)
    eye4 = np.tile(eye, (256 // chan, 1))
    tables = {
        "kz_all": kz_all,
        "ay": const(ay),
        "ax": const(ax),
        "axt": const(ax.transpose(0, 2, 1)),
        "ayt": const(ay.transpose(0, 2, 1)),
        "rep": const(rep),
        "mask": jnp.asarray(mask),
        "fold": const(fold),
        "spread": const(spread),
        "sum_o": const(sum_o),
        "eye": const(eye4),
    }
    rows = cx * cy
    brow = qy * cx
    n_a = ny * nx

    def call(first, ins):
        args = dict(ins, **tables)
        t = 1 if first else 3
        outs = {
            "down": jax.ShapeDtypeStruct((rows, lanes), bf16 if first else f32),
            "hat": jax.ShapeDtypeStruct((modes, 2 * chan), f32),
        }
        if first:
            outs["pt"] = jax.ShapeDtypeStruct((chan, 2 * chan), f32)
        else:
            outs["hat_in_one"] = jax.ShapeDtypeStruct((modes, 2 * chan), f32)
            outs["hat_in_two"] = jax.ShapeDtypeStruct((modes, 2 * chan), f32)
        scratch = {
            "y": pltpu.VMEM((t, MY * cx, MZ * chan), f32),
            "land_a": pltpu.VMEM((t, 2, n_a, brow, blane // 2), f32),
            "p": pltpu.VMEM((t, 2, nz, mrow, blane // 2), f32),
            "land_b": pltpu.VMEM((t, 2, nz, mrow, blane // 2), f32),
            "c": pltpu.VMEM((2, nz, mrow, blane // 2), f32),
            "cat": pltpu.VMEM((nz * mrow, blane // 2), f32),
            "v": pltpu.VMEM((MY * cx, MZ * chan), f32),
            "v2": pltpu.VMEM((rows, MZ * chan), bf16),
            "kz": pltpu.VMEM((lanes, MZ * chan), bf16),
            "kz_sem": pltpu.SemaphoreType.DMA((2 * nx,)),
            "p4": pltpu.VMEM((256, 256), bf16),
        }
        sems = {"c": nz, "d": n_a}
        for k in range(t):
            sems["a%d" % k] = n_a
            sems["b%d" % k] = nz
        if first:
            scratch["pt_a"] = pltpu.VMEM((n_a, chan, 2 * chan), f32)
            scratch["pt_b"] = pltpu.VMEM((nz, chan, 2 * chan), f32)
            sems["pa"] = n_a
            sems["pb"] = nz
        for k, n in sems.items():
            scratch[k + "_s"] = pltpu.SemaphoreType.DMA((2, n))
            scratch[k + "_r"] = pltpu.SemaphoreType.DMA((2, n))
        cfg = dict(
            nz=nz, ny=ny, nx=nx, first=first, brow=brow, blane=blane, mrow=mrow,
            scales=(a_scale, b_scale), chan=chan,
            names=list(args) + list(outs) + list(scratch),
        )
        vmem = pl.BlockSpec(memory_space=pltpu.VMEM)
        got = pl.pallas_call(
            functools.partial(layer_kernel, cfg),
            out_shape=list(outs.values()),
            in_specs=[
                pl.BlockSpec(memory_space=pltpu.HBM) if k == "kz_all" else vmem for k in args
            ],
            out_specs=[vmem] * len(outs),
            scratch_shapes=list(scratch.values()),
            compiler_params=pltpu.CompilerParams(
                collective_id=1 if first else 0,
                has_side_effects=True,
                vmem_limit_bytes=48 * 1024 * 1024,
            ),
            name="layer_one" if first else "layer_two",
        )(*args.values())
        return dict(zip(outs, got))

    flat = (rows, lanes)
    gin = grid_input.reshape(flat)
    value_one, slope_one = gelu_both(pre_one.reshape(flat).astype(f32))
    _, slope_two = gelu_both(pre_two.reshape(flat).astype(f32))
    mid = value_one.astype(bf16)
    dz_two = (grad_output.reshape(flat).astype(f32) * slope_two).astype(bf16)
    two = call(
        False,
        {
            "dz": dz_two,
            "mid": mid,
            "gin": gin,
            "weights": spectral_two.reshape(modes, chan * chan),
            "point": point_two,
        },
    )
    dz_one = (two["down"] * slope_one).astype(bf16)
    one = call(
        True,
        {
            "dz": dz_one,
            "mid": mid,
            "gin": gin,
            "dz_two": dz_two,
            "weights": spectral_one.reshape(modes, chan * chan),
            "point": point_one,
        },
    )
    step = 1024
    small = pl.BlockSpec((modes, 2 * chan), lambda n: (0, 0))
    large = pl.BlockSpec((modes, step), lambda n: (0, n))
    spec_one, spec_two = pl.pallas_call(
        functools.partial(outer_kernel, chan),
        grid=(chan * chan // step,),
        out_shape=[jax.ShapeDtypeStruct((modes, chan * chan), f32)] * 2,
        in_specs=[small] * 4 + [pl.BlockSpec((step, chan), lambda n: (n, 0))],
        out_specs=[large] * 2,
        name="outer",
    )(two["hat_in_one"], one["hat"], two["hat_in_two"], two["hat"], tables["sum_o"])
    return (
        one["down"].reshape(grid_input.shape),
        spec_one.reshape(spectral_one.shape),
        spec_two.reshape(spectral_two.shape),
        one["pt"][:, chan:],
        one["pt"][:, :chan],
    )


def solution(mesh):
    grid = P("gz", "gy", "gx")
    spec = P("gz", "gy", "gx", None)
    return jax.shard_map(
        on_device,
        mesh=mesh,
        in_specs=(grid, grid, grid, grid, spec, spec, P(), P()),
        out_specs=(grid, spec, spec, P(), P()),
        check_vma=False,
    )
```

```python
import functools
import math

import jax
import jax.numpy as jnp
import ml_dtypes
import numpy as np
from jax import lax
from jax.experimental import pallas as pl
from jax.experimental.pallas import tpu as pltpu
from jax.sharding import PartitionSpec as P

MX = 16
MY = 16
MZ = 16

inv_root_two = 0.7071067811865476
inv_root_tau = 0.3989422804014327
bf16 = jnp.bfloat16
f32 = jnp.float32


def cas_tables(mode_count, cells, devices):
    length = cells * devices
    mode = np.arange(mode_count)
    frequency = np.where(mode < mode_count // 2, mode, length - mode_count + mode)
    position = np.arange(cells)[None, :] * devices + np.arange(devices)[:, None]
    product = (frequency[None, :, None] * position[:, None, :]) % length
    phase = product.astype(np.float32) * np.float32(2.0 * math.pi / length)
    return (np.cos(phase) + np.sin(phase)).astype(ml_dtypes.bfloat16).astype(np.float32)


def const(values):
    return jnp.asarray(np.asarray(values).astype(ml_dtypes.bfloat16))


def gelu_both(pre_value):
    cdf = 0.5 * (1.0 + lax.erf(pre_value * inv_root_two))
    slope = cdf + pre_value * jnp.exp(-0.5 * pre_value * pre_value) * inv_root_tau
    return pre_value * cdf, slope


def mm(a, b):
    return jnp.dot(a.astype(bf16), b.astype(bf16), preferred_element_type=f32)


def mm_t(a, b):
    return lax.dot_general(
        a.astype(bf16), b.astype(bf16), (((1,), (1,)), ((), ())), preferred_element_type=f32
    )


def tmm(a, b):
    return lax.dot_general(
        a.astype(bf16), b.astype(bf16), (((0,), (0,)), ((), ())), preferred_element_type=f32
    )


def layer_kernel(cfg, *refs):
    nz, ny, nx = cfg["nz"], cfg["ny"], cfg["nx"]
    first = cfg["first"]
    brow, blane = cfg["brow"], cfg["blane"]
    mrow = cfg["mrow"]
    a_scale, b_scale = cfg["scales"]
    chan = cfg["chan"]
    n_a = ny * nx
    names = cfg["names"]
    r = dict(zip(names, refs))
    kz = r["kz"]

    def table(name, index=None):
        start, (count, rows, cols) = cfg["places"][name]
        if index is None:
            return r["pack"][start : start + rows, :cols]
        return r["pack"][pl.ds(pl.multiple_of(start + index * rows, 16), rows), :cols]

    modes = mrow * blane // chan
    mask = lax.rem(
        lax.broadcasted_iota(jnp.int32, (modes, blane), 0), blane // chan
    ) == lax.div(lax.broadcasted_iota(jnp.int32, (modes, blane), 1), chan)
    half = blane // 2
    gz, gy, gx = lax.axis_index("gz"), lax.axis_index("gy"), lax.axis_index("gx")

    def wrap(v, n):
        return lax.rem(v, n)

    def a_peer(j):
        return wrap(gy + j // nx, ny), wrap(gx + j % nx, nx)

    def a_device(j):
        py, px = a_peer(j)
        return (gz, py, px)

    def b_device(j):
        return (wrap(gz + j, nz), gy, gx)

    width = kz.shape[1]
    tile = 256
    lanes = kz.shape[0]
    loads = {}
    for h in range(2):
        for px in range(nx):
            n = 2 * px + h
            cols = slice(n * half, (n + 1) * half)
            loads[n] = pltpu.make_async_copy(
                r["kz_all"].at[gx, :, cols], kz.at[:, cols], r["kz_sem"].at[n]
            )
            loads[n].start()

    barrier = pltpu.get_barrier_semaphore()
    for j in range(1, n_a):
        pl.semaphore_signal(barrier, 1, device_id=a_device(j), device_id_type=pl.DeviceIdType.MESH)
    for j in range(1, nz):
        pl.semaphore_signal(barrier, 1, device_id=b_device(j), device_id_type=pl.DeviceIdType.MESH)

    copies = []

    def remote(src, dst, sem, j, dev, h=0):
        c = pltpu.make_async_remote_copy(
            src_ref=src, dst_ref=dst,
            send_sem=r[sem + "_s"].at[h, j], recv_sem=r[sem + "_r"].at[h, j],
            device_id=dev, device_id_type=pl.DeviceIdType.MESH,
        )
        c.start()
        copies.append(c)
        return c

    def analyse(src, t):
        table_y = table("ay", gy)

        def body(n, carry):
            cols = pl.ds(pl.multiple_of(n * tile, tile), tile)
            part = mm(src[...], kz[:, cols])
            r["y"][t, :, cols] = mm(table_y, part)
            return carry

        lax.fori_loop(0, width // tile, body, 0)

    def block(py, px, h=None):
        size = blane if h is None else half
        return (
            pl.ds(pl.multiple_of(py * brow, brow), brow),
            pl.ds(pl.multiple_of(px * blane + (h or 0) * half, half), size),
        )

    a_order = sorted(range(1, n_a), key=lambda j: (j % nx == 0, j))

    def start_a(t, h):
        out = []
        for j in a_order:
            rows, cols = block(*a_peer(j), h)
            out.append(
                remote(
                    r["y"].at[t, rows, cols], r["land_a"].at[t, h, j], "a%d" % t, j, a_device(j), h
                )
            )
        return out

    def finish_a(t, cs):
        out = []
        for h in range(2):
            rows, cols = block(gy, gx, h)
            for c in cs[h]:
                c.wait_recv()
            total = r["y"][t, rows, cols]
            for j in range(1, n_a):
                total = total + r["land_a"][t, h, j]
            part = mm(table("ax", gz), total)
            for s in range(nz):
                r["p"][t, h, s] = part[s * mrow : (s + 1) * mrow, :]
            for j in range(1, nz):
                dev = b_device(j)
                out.append(
                    remote(r["p"].at[t, h, dev[0]], r["land_b"].at[t, h, j], "b%d" % t, j, dev, h)
                )
        return out

    def finish_b(t, cs, scale):
        for c in cs:
            c.wait_recv()
        parts = []
        for h in range(2):
            total = r["p"][t, h, gz]
            for j in range(1, nz):
                total = total + r["land_b"][t, h, j]
            parts.append(total)
        total = jnp.concatenate(parts, axis=1)
        spread = jnp.where(mask, mm(table("rep"), total * scale), 0.0)
        return mm(spread, table("fold"))

    wait_a = []
    for h in range(2):
        for px in range(nx):
            n = 2 * px + h
            cols = slice(n * half, (n + 1) * half)
            loads[n].wait()
            r["y"][0, :, cols] = mm(table("ay", gy), mm(r["dz"][...], kz[:, cols]))
        if h == 0:
            pl.semaphore_wait(barrier, n_a + nz - 2)
        wait_a.append(start_a(0, h))
    if first:
        lane = lax.broadcasted_iota(jnp.int32, (chan, 2 * chan), 1)

        def point_part(left, right):
            total = jnp.zeros((2 * chan, 2 * chan), f32)

            def body(n, acc):
                cols = pl.ds(pl.multiple_of(n * 2 * chan, 2 * chan), 2 * chan)
                return acc + tmm(left[:, cols], right[:, cols])

            return lax.fori_loop(0, lanes // (2 * chan), body, total)

        pa = point_part(r["mid"], r["dz_two"])
        pb = point_part(r["gin"], r["dz"])
        low = lane < chan
        keep = jnp.where(low, pa[:chan], pb[chan:])
        turn = jnp.where(low, pb[:chan], pa[chan:])
        r["pt_a"][gy * nx + gx] = keep + pltpu.roll(turn, chan, 1)
        wait_pa = [
            remote(
                r["pt_a"].at[gy * nx + gx], r["pt_a"].at[gy * nx + gx], "pa", j, a_device(j)
            )
            for j in range(1, n_a)
        ]
    else:
        analyse(r["mid"], 1)
        wait_a1 = [start_a(1, 0), start_a(1, 1)]
        analyse(r["gin"], 2)
        wait_a2 = [start_a(2, 0), start_a(2, 1)]
    wait_b = finish_a(0, wait_a)
    tall = mm_t(table("eye"), r["point"][...])
    square = mm_t(tall, table("eye"))
    row_i = lax.broadcasted_iota(jnp.int32, square.shape, 0) // chan
    col_i = lax.broadcasted_iota(jnp.int32, square.shape, 1) // chan
    r["p4"][...] = jnp.where(row_i == col_i, square, 0.0).astype(bf16)
    if first:
        for c in wait_pa:
            c.wait_recv()
        total = r["pt_a"][0]
        for j in range(1, n_a):
            total = total + r["pt_a"][j]
        r["pt_b"][gz] = total
        wait_pb = [
            remote(r["pt_b"].at[gz], r["pt_b"].at[gz], "pb", j, b_device(j))
            for j in range(1, nz)
        ]
    hat = finish_b(0, wait_b, b_scale)
    wide = r["weights"].shape[1]
    prod_tile = jnp.concatenate([hat] * (512 // hat.shape[1]), axis=1)
    back = jnp.zeros((hat.shape[0], chan), f32)
    for n in range(wide // 512):
        w = r["weights"][:, n * 512 : (n + 1) * 512].astype(f32)
        back = back + mm(w * prod_tile, r["sum_o"][n * 512 : (n + 1) * 512, :])
    spread = jnp.where(mask, mm_t(back, table("fold")[:, :chan]), 0.0)
    mixed = tmm(table("rep"), spread)
    wait_c = []
    for h in range(2):
        r["c"][h, gz] = mixed[:, h * half : (h + 1) * half]
        wait_c.append(
            [
                remote(r["c"].at[h, gz], r["c"].at[h, gz], "c", j, b_device(j), h)
                for j in range(1, nz)
            ]
        )
    if not first:
        wait_b1 = finish_a(1, wait_a1)
        wait_b2 = finish_a(2, wait_a2)
    wait_d = []
    for h in range(2):
        for c in wait_c[h]:
            c.wait_recv()
        for s in range(nz):
            r["cat"][s * mrow : (s + 1) * mrow, :] = r["c"][h, s]
        rows, cols = block(gy, gx, h)
        r["v"][rows, cols] = mm(table("axt", gz), r["cat"][...])
        wait_d += [
            remote(r["v"].at[rows, cols], r["v"].at[rows, cols], "d", j, a_device(j), h)
            for j in a_order
        ]
    r["hat"][0] = hat
    if not first:
        r["hat"][1] = finish_b(1, wait_b1, a_scale)
        r["hat"][2] = finish_b(2, wait_b2, a_scale)
    if first:
        for c in wait_pb:
            c.wait_recv()
        total = r["pt_b"][0]
        for j in range(1, nz):
            total = total + r["pt_b"][j]
        r["pt"][...] = total * b_scale
    for c in wait_d:
        c.wait_recv()
    r["v2"][...] = (mm(table("ayt", gy), r["v"][...]) * a_scale).astype(bf16)

    def body(n, carry):
        cs = pl.ds(pl.multiple_of(n * tile, tile), tile)
        r["down"][:, cs] = (
            mm_t(r["v2"][...], kz[cs, :]) + mm(r["dz"][:, cs], r["p4"][...])
        ).astype(r["down"].dtype)
        return carry

    lax.fori_loop(0, lanes // tile, body, 0)
    for c in copies:
        c.wait_send()


def outer_kernel(chan, hat_one, hat_two, sum_o, spec_one, spec_two):
    for hat_in, hat, out in (
        (hat_two[2], hat_one[0], spec_one),
        (hat_two[1], hat_two[0], spec_two),
    ):
        times = out.shape[1] // hat.shape[1]
        out[...] = mm_t(hat_in[:, :chan], sum_o[...]) * jnp.concatenate([hat] * times, axis=1)


def on_device(
    grid_input, pre_one, pre_two, grad_output, spectral_one, spectral_two, point_one, point_two
):
    chan = point_one.shape[0]
    nz, ny, nx = (lax.axis_size("gz"), lax.axis_size("gy"), lax.axis_size("gx"))
    cx, cy = grid_input.shape[:2]
    lanes = grid_input.shape[2]
    cz = lanes // chan
    qx, qy, qz = MX // nz, MY // ny, MZ // nx
    total_cells = cx * nz * cy * ny * cz * nx
    b_scale = total_cells ** (-0.5)
    a_scale = (total_cells * MX * MY * MZ) ** (-0.25)
    tx, ty, tz = cas_tables(MX, cx, nz), cas_tables(MY, cy, ny), cas_tables(MZ, cz, nx)
    eye = np.eye(chan, dtype=np.float32)
    kz_all = np.zeros((nx, cz, chan, MZ, chan), ml_dtypes.bfloat16)
    diag = np.arange(chan)
    kz_all[:, :, diag, :, diag] = tz.transpose(0, 2, 1).astype(ml_dtypes.bfloat16)[None]
    kz_all = const(kz_all.reshape(nx, lanes, MZ * chan))
    ay = np.einsum("dky,xw->dkxwy", ty, np.eye(cx)).reshape(ny, MY * cx, cx * cy)
    ax = np.einsum("dkx,ab->dkabx", tx, np.eye(qy)).reshape(nz, MX * qy, qy * cx)
    modes = qx * qy * qz
    mrow = qx * qy
    blane = qz * chan
    mode = np.arange(modes)
    rep = (mode[:, None] // qz == np.arange(mrow)[None, :]).astype(np.float32)
    fold = np.tile(np.concatenate([eye, eye], axis=1), (qz, 1))
    sum_o = np.repeat(eye, chan, axis=0)
    eye4 = np.tile(eye, (256 // chan, 1))
    pieces = {
        "ay": ay,
        "ax": ax,
        "axt": ax.transpose(0, 2, 1),
        "ayt": ay.transpose(0, 2, 1),
        "rep": rep[None],
        "fold": fold[None],
        "eye": eye4[None],
    }
    places, packed, start = {}, [], 0
    pack_cols = max(v.shape[2] for v in pieces.values())
    for k, v in pieces.items():
        assert v.shape[1] % 16 == 0
        places[k] = (start, v.shape)
        start += v.shape[0] * v.shape[1]
        flat_rows = v.reshape(-1, v.shape[2])
        packed.append(np.pad(flat_rows, ((0, 0), (0, pack_cols - v.shape[2]))))
    tables = {
        "kz_all": kz_all,
        "pack": const(np.concatenate(packed)),
        "sum_o": const(sum_o),
    }
    rows = cx * cy
    brow = qy * cx
    n_a = ny * nx

    def call(first, ins):
        args = dict(ins, **tables)
        t = 1 if first else 3
        outs = {
            "down": jax.ShapeDtypeStruct((rows, lanes), bf16 if first else f32),
            "hat": jax.ShapeDtypeStruct((t, modes, 2 * chan), f32),
        }
        if first:
            outs["pt"] = jax.ShapeDtypeStruct((chan, 2 * chan), f32)
        scratch = {
            "y": pltpu.VMEM((t, MY * cx, MZ * chan), f32),
            "land_a": pltpu.VMEM((t, 2, n_a, brow, blane // 2), f32),
            "p": pltpu.VMEM((t, 2, nz, mrow, blane // 2), f32),
            "land_b": pltpu.VMEM((t, 2, nz, mrow, blane // 2), f32),
            "c": pltpu.VMEM((2, nz, mrow, blane // 2), f32),
            "cat": pltpu.VMEM((nz * mrow, blane // 2), f32),
            "v": pltpu.VMEM((MY * cx, MZ * chan), f32),
            "v2": pltpu.VMEM((rows, MZ * chan), bf16),
            "kz": pltpu.VMEM((lanes, MZ * chan), bf16),
            "kz_sem": pltpu.SemaphoreType.DMA((2 * nx,)),
            "p4": pltpu.VMEM((256, 256), bf16),
        }
        sems = {"c": nz, "d": n_a}
        for k in range(t):
            sems["a%d" % k] = n_a
            sems["b%d" % k] = nz
        if first:
            scratch["pt_a"] = pltpu.VMEM((n_a, chan, 2 * chan), f32)
            scratch["pt_b"] = pltpu.VMEM((nz, chan, 2 * chan), f32)
            sems["pa"] = n_a
            sems["pb"] = nz
        for k, n in sems.items():
            scratch[k + "_s"] = pltpu.SemaphoreType.DMA((2, n))
            scratch[k + "_r"] = pltpu.SemaphoreType.DMA((2, n))
        cfg = dict(
            places=places,
            nz=nz, ny=ny, nx=nx, first=first, brow=brow, blane=blane, mrow=mrow,
            scales=(a_scale, b_scale), chan=chan,
            names=list(args) + list(outs) + list(scratch),
        )
        vmem = pl.BlockSpec(memory_space=pltpu.VMEM)
        got = pl.pallas_call(
            functools.partial(layer_kernel, cfg),
            out_shape=list(outs.values()),
            in_specs=[
                pl.BlockSpec(memory_space=pltpu.HBM) if k == "kz_all" else vmem
                for k in args
            ],
            out_specs=[vmem] * len(outs),
            scratch_shapes=list(scratch.values()),
            compiler_params=pltpu.CompilerParams(
                collective_id=1 if first else 0,
                has_side_effects=True,
                vmem_limit_bytes=48 * 1024 * 1024,
            ),
            name="layer_one" if first else "layer_two",
        )(*args.values())
        return dict(zip(outs, got))

    flat = (rows, lanes)
    gin = grid_input.reshape(flat)
    value_one, slope_one = gelu_both(pre_one.reshape(flat).astype(f32))
    _, slope_two = gelu_both(pre_two.reshape(flat).astype(f32))
    mid = value_one.astype(bf16)
    dz_two = (grad_output.reshape(flat).astype(f32) * slope_two).astype(bf16)
    two = call(
        False,
        {
            "dz": dz_two,
            "mid": mid,
            "gin": gin,
            "weights": spectral_two.reshape(modes, chan * chan),
            "point": point_two,
        },
    )
    dz_one = (two["down"] * slope_one).astype(bf16)
    one = call(
        True,
        {
            "dz": dz_one,
            "mid": mid,
            "gin": gin,
            "dz_two": dz_two,
            "weights": spectral_one.reshape(modes, chan * chan),
            "point": point_one,
        },
    )
    step = 1024
    small = [pl.BlockSpec((t, modes, 2 * chan), lambda n: (0, 0, 0)) for t in (1, 3)]
    large = pl.BlockSpec((modes, step), lambda n: (0, n))
    spec_one, spec_two = pl.pallas_call(
        functools.partial(outer_kernel, chan),
        grid=(chan * chan // step,),
        out_shape=[jax.ShapeDtypeStruct((modes, chan * chan), f32)] * 2,
        in_specs=small + [pl.BlockSpec((step, chan), lambda n: (n, 0))],
        out_specs=[large] * 2,
        name="outer",
    )(one["hat"], two["hat"], tables["sum_o"])
    return (
        one["down"].reshape(grid_input.shape),
        spec_one.reshape(spectral_one.shape),
        spec_two.reshape(spectral_two.shape),
        one["pt"][:, chan:],
        one["pt"][:, :chan],
    )


def solution(mesh):
    grid = P("gz", "gy", "gx")
    spec = P("gz", "gy", "gx", None)
    return jax.shard_map(
        on_device,
        mesh=mesh,
        in_specs=(grid, grid, grid, grid, spec, spec, P(), P()),
        out_specs=(grid, spec, spec, P(), P()),
        check_vma=False,
    )
```

```python
import functools
import math

import jax
import jax.numpy as jnp
import ml_dtypes
import numpy as np
from jax import lax
from jax.experimental import pallas as pl
from jax.experimental.pallas import tpu as pltpu
from jax.sharding import PartitionSpec as P

MX = 16
MY = 16
MZ = 16

inv_root_two = 0.7071067811865476
inv_root_tau = 0.3989422804014327
bf16 = jnp.bfloat16
f32 = jnp.float32


def cas_tables(mode_count, cells, devices):
    length = cells * devices
    mode = np.arange(mode_count)
    frequency = np.where(mode < mode_count // 2, mode, length - mode_count + mode)
    position = np.arange(cells)[None, :] * devices + np.arange(devices)[:, None]
    product = (frequency[None, :, None] * position[:, None, :]) % length
    phase = product.astype(np.float32) * np.float32(2.0 * math.pi / length)
    return (np.cos(phase) + np.sin(phase)).astype(ml_dtypes.bfloat16).astype(np.float32)


def const(values):
    return jnp.asarray(np.asarray(values).astype(ml_dtypes.bfloat16))


def gelu_both(pre_value):
    cdf = 0.5 * (1.0 + lax.erf(pre_value * inv_root_two))
    slope = cdf + pre_value * jnp.exp(-0.5 * pre_value * pre_value) * inv_root_tau
    return pre_value * cdf, slope


def mm(a, b):
    return jnp.dot(a.astype(bf16), b.astype(bf16), preferred_element_type=f32)


def mm_t(a, b):
    return lax.dot_general(
        a.astype(bf16), b.astype(bf16), (((1,), (1,)), ((), ())), preferred_element_type=f32
    )


def tmm(a, b):
    return lax.dot_general(
        a.astype(bf16), b.astype(bf16), (((0,), (0,)), ((), ())), preferred_element_type=f32
    )


def layer_kernel(cfg, *refs):
    nz, ny, nx = cfg["nz"], cfg["ny"], cfg["nx"]
    first = cfg["first"]
    brow, blane = cfg["brow"], cfg["blane"]
    mrow = cfg["mrow"]
    a_scale, b_scale = cfg["scales"]
    chan = cfg["chan"]
    n_a = ny * nx
    names = cfg["names"]
    r = dict(zip(names, refs))
    kz = r["kz"]

    def table(name, index=None):
        start, (count, rows, cols) = cfg["places"][name]
        if index is None:
            return r["pack"][start : start + rows, :cols]
        return r["pack"][pl.ds(pl.multiple_of(start + index * rows, 16), rows), :cols]

    modes = mrow * blane // chan
    mask = lax.rem(
        lax.broadcasted_iota(jnp.int32, (modes, blane), 0), blane // chan
    ) == lax.div(lax.broadcasted_iota(jnp.int32, (modes, blane), 1), chan)
    half = blane // 2
    gz, gy, gx = lax.axis_index("gz"), lax.axis_index("gy"), lax.axis_index("gx")

    def wrap(v, n):
        return lax.rem(v, n)

    def a_peer(j):
        return wrap(gy + j // nx, ny), wrap(gx + j % nx, nx)

    def a_device(j):
        py, px = a_peer(j)
        return (gz, py, px)

    def b_device(j):
        return (wrap(gz + j, nz), gy, gx)

    width = kz.shape[1]
    tile = 256
    lanes = kz.shape[0]
    loads = {}
    for h in range(2):
        for px in range(nx):
            n = 2 * px + h
            cols = slice(n * half, (n + 1) * half)
            loads[n] = pltpu.make_async_copy(
                r["kz_all"].at[gx, :, cols], kz.at[:, cols], r["kz_sem"].at[n]
            )
            loads[n].start()

    barrier = pltpu.get_barrier_semaphore()
    for j in range(1, n_a):
        pl.semaphore_signal(barrier, 1, device_id=a_device(j), device_id_type=pl.DeviceIdType.MESH)
    for j in range(1, nz):
        pl.semaphore_signal(barrier, 1, device_id=b_device(j), device_id_type=pl.DeviceIdType.MESH)

    copies = []

    def remote(src, dst, sem, j, dev, h=0):
        c = pltpu.make_async_remote_copy(
            src_ref=src, dst_ref=dst,
            send_sem=r[sem + "_s"].at[h, j], recv_sem=r[sem + "_r"].at[h, j],
            device_id=dev, device_id_type=pl.DeviceIdType.MESH,
        )
        c.start()
        copies.append(c)
        return c

    def analyse(src, t):
        table_y = table("ay", gy)

        def body(n, carry):
            cols = pl.ds(pl.multiple_of(n * tile, tile), tile)
            part = mm(src[...], kz[:, cols])
            r["y"][t, :, cols] = mm(table_y, part)
            return carry

        lax.fori_loop(0, width // tile, body, 0)

    def block(py, px, h=None):
        size = blane if h is None else half
        return (
            pl.ds(pl.multiple_of(py * brow, brow), brow),
            pl.ds(pl.multiple_of(px * blane + (h or 0) * half, half), size),
        )

    def start_a(t, h):
        out = {}
        for dx in list(range(1, nx)) + [0]:
            for dy in range(1, ny):
                j = dy * nx + dx
                rows, cols = block(*a_peer(j), h)
                out[j] = remote(
                    r["y"].at[t, rows, cols], r["land_a"].at[t, h, j], "a%d" % t, j,
                    a_device(dy * nx), h,
                )
        return out

    def middle_a(t, cs):
        for h in range(2):
            for dx in range(1, nx):
                rows, cols = block(*a_peer(dx), h)
                total = r["y"][t, rows, cols]
                for dy in range(1, ny):
                    j = dy * nx + dx
                    cs[h].pop(j).wait_recv()
                    total = total + r["land_a"][t, h, j]
                r["y"][t, rows, cols] = total
                cs[h][dx] = remote(
                    r["y"].at[t, rows, cols], r["land_a"].at[t, h, dx], "a%d" % t, dx,
                    a_device(dx), h,
                )

    def finish_a(t, cs):
        out = []
        for h in range(2):
            rows, cols = block(gy, gx, h)
            total = r["y"][t, rows, cols]
            for j, c in cs[h].items():
                c.wait_recv()
                total = total + r["land_a"][t, h, j]
            part = mm(table("ax", gz), total)
            for s in range(nz):
                r["p"][t, h, s] = part[s * mrow : (s + 1) * mrow, :]
            for j in range(1, nz):
                dev = b_device(j)
                out.append(
                    remote(r["p"].at[t, h, dev[0]], r["land_b"].at[t, h, j], "b%d" % t, j, dev, h)
                )
        return out

    def finish_b(t, cs, scale):
        for c in cs:
            c.wait_recv()
        parts = []
        for h in range(2):
            total = r["p"][t, h, gz]
            for j in range(1, nz):
                total = total + r["land_b"][t, h, j]
            parts.append(total)
        total = jnp.concatenate(parts, axis=1)
        spread = jnp.where(mask, mm(table("rep"), total * scale), 0.0)
        return mm(spread, table("fold"))

    wait_a = []
    for h in range(2):
        for px in range(nx):
            n = 2 * px + h
            cols = slice(n * half, (n + 1) * half)
            loads[n].wait()
            r["y"][0, :, cols] = mm(table("ay", gy), mm(r["dz"][...], kz[:, cols]))
        if h == 0:
            pl.semaphore_wait(barrier, n_a + nz - 2)
        wait_a.append(start_a(0, h))
    middle_a(0, wait_a)
    if first:
        lane = lax.broadcasted_iota(jnp.int32, (chan, 2 * chan), 1)

        def point_part(left, right):
            total = jnp.zeros((2 * chan, 2 * chan), f32)

            def body(n, acc):
                cols = pl.ds(pl.multiple_of(n * 2 * chan, 2 * chan), 2 * chan)
                return acc + tmm(left[:, cols], right[:, cols])

            return lax.fori_loop(0, lanes // (2 * chan), body, total)

        pa = point_part(r["mid"], r["dz_two"])
        pb = point_part(r["gin"], r["dz"])
        low = lane < chan
        keep = jnp.where(low, pa[:chan], pb[chan:])
        turn = jnp.where(low, pb[:chan], pa[chan:])
        r["pt_a"][gy * nx + gx] = keep + pltpu.roll(turn, chan, 1)
        wait_pa = [
            remote(
                r["pt_a"].at[gy * nx + gx], r["pt_a"].at[gy * nx + gx], "pa", j, a_device(j)
            )
            for j in range(1, n_a)
        ]
    else:
        analyse(r["mid"], 1)
        wait_a1 = [start_a(1, 0), start_a(1, 1)]
        analyse(r["gin"], 2)
        wait_a2 = [start_a(2, 0), start_a(2, 1)]
    wait_b = finish_a(0, wait_a)
    if not first:
        middle_a(1, wait_a1)
        middle_a(2, wait_a2)
    tall = mm_t(table("eye"), r["point"][...])
    square = mm_t(tall, table("eye"))
    row_i = lax.broadcasted_iota(jnp.int32, square.shape, 0) // chan
    col_i = lax.broadcasted_iota(jnp.int32, square.shape, 1) // chan
    r["p4"][...] = jnp.where(row_i == col_i, square, 0.0).astype(bf16)
    if first:
        for c in wait_pa:
            c.wait_recv()
        total = r["pt_a"][0]
        for j in range(1, n_a):
            total = total + r["pt_a"][j]
        r["pt_b"][gz] = total
        wait_pb = [
            remote(r["pt_b"].at[gz], r["pt_b"].at[gz], "pb", j, b_device(j))
            for j in range(1, nz)
        ]
    hat = finish_b(0, wait_b, b_scale)
    wide = r["weights"].shape[1]
    prod_tile = jnp.concatenate([hat] * (512 // hat.shape[1]), axis=1)
    back = jnp.zeros((hat.shape[0], chan), f32)
    for n in range(wide // 512):
        w = r["weights"][:, n * 512 : (n + 1) * 512].astype(f32)
        back = back + mm(w * prod_tile, r["sum_o"][n * 512 : (n + 1) * 512, :])
    spread = jnp.where(mask, mm_t(back, table("fold")[:, :chan]), 0.0)
    mixed = tmm(table("rep"), spread)
    wait_c = []
    for h in range(2):
        r["c"][h, gz] = mixed[:, h * half : (h + 1) * half]
        wait_c.append(
            [
                remote(r["c"].at[h, gz], r["c"].at[h, gz], "c", j, b_device(j), h)
                for j in range(1, nz)
            ]
        )
    if not first:
        wait_b1 = finish_a(1, wait_a1)
        wait_b2 = finish_a(2, wait_a2)
    wait_d = []
    for h in range(2):
        for c in wait_c[h]:
            c.wait_recv()
        for s in range(nz):
            r["cat"][s * mrow : (s + 1) * mrow, :] = r["c"][h, s]
        rows, cols = block(gy, gx, h)
        r["v"][rows, cols] = mm(table("axt", gz), r["cat"][...])
        direct = {}
        for j in list(range(1, nx)) + [dy * nx for dy in range(1, ny)]:
            direct[j] = remote(
                r["v"].at[rows, cols], r["v"].at[rows, cols], "d", j, a_device(j), h
            )
        wait_d.append(direct)
    for h in range(2):
        for dx in range(1, nx):
            wait_d[h].pop(dx).wait_recv()
            rows, cols = block(gy, wrap(gx + nx - dx, nx), h)
            for dy in range(1, ny):
                j = dy * nx + dx
                wait_d[h][j] = remote(
                    r["v"].at[rows, cols], r["v"].at[rows, cols], "d", j, a_device(dy * nx), h
                )
    r["hat"][0] = hat
    if not first:
        r["hat"][1] = finish_b(1, wait_b1, a_scale)
        r["hat"][2] = finish_b(2, wait_b2, a_scale)
    if first:
        for c in wait_pb:
            c.wait_recv()
        total = r["pt_b"][0]
        for j in range(1, nz):
            total = total + r["pt_b"][j]
        r["pt"][...] = total * b_scale
    for h in range(2):
        for c in wait_d[h].values():
            c.wait_recv()
    r["v2"][...] = (mm(table("ayt", gy), r["v"][...]) * a_scale).astype(bf16)

    def body(n, carry):
        cs = pl.ds(pl.multiple_of(n * tile, tile), tile)
        r["down"][:, cs] = (
            mm_t(r["v2"][...], kz[cs, :]) + mm(r["dz"][:, cs], r["p4"][...])
        ).astype(r["down"].dtype)
        return carry

    lax.fori_loop(0, lanes // tile, body, 0)
    for c in copies:
        c.wait_send()


def outer_kernel(chan, hat_one, hat_two, sum_o, spec_one, spec_two):
    for hat_in, hat, out in (
        (hat_two[2], hat_one[0], spec_one),
        (hat_two[1], hat_two[0], spec_two),
    ):
        times = out.shape[1] // hat.shape[1]
        out[...] = mm_t(hat_in[:, :chan], sum_o[...]) * jnp.concatenate([hat] * times, axis=1)


def on_device(
    grid_input, pre_one, pre_two, grad_output, spectral_one, spectral_two, point_one, point_two
):
    chan = point_one.shape[0]
    nz, ny, nx = (lax.axis_size("gz"), lax.axis_size("gy"), lax.axis_size("gx"))
    cx, cy = grid_input.shape[:2]
    lanes = grid_input.shape[2]
    cz = lanes // chan
    qx, qy, qz = MX // nz, MY // ny, MZ // nx
    total_cells = cx * nz * cy * ny * cz * nx
    b_scale = total_cells ** (-0.5)
    a_scale = (total_cells * MX * MY * MZ) ** (-0.25)
    tx, ty, tz = cas_tables(MX, cx, nz), cas_tables(MY, cy, ny), cas_tables(MZ, cz, nx)
    eye = np.eye(chan, dtype=np.float32)
    kz_all = np.zeros((nx, cz, chan, MZ, chan), ml_dtypes.bfloat16)
    diag = np.arange(chan)
    kz_all[:, :, diag, :, diag] = tz.transpose(0, 2, 1).astype(ml_dtypes.bfloat16)[None]
    kz_all = const(kz_all.reshape(nx, lanes, MZ * chan))
    ay = np.einsum("dky,xw->dkxwy", ty, np.eye(cx)).reshape(ny, MY * cx, cx * cy)
    ax = np.einsum("dkx,ab->dkabx", tx, np.eye(qy)).reshape(nz, MX * qy, qy * cx)
    modes = qx * qy * qz
    mrow = qx * qy
    blane = qz * chan
    mode = np.arange(modes)
    rep = (mode[:, None] // qz == np.arange(mrow)[None, :]).astype(np.float32)
    fold = np.tile(np.concatenate([eye, eye], axis=1), (qz, 1))
    sum_o = np.repeat(eye, chan, axis=0)
    eye4 = np.tile(eye, (256 // chan, 1))
    pieces = {
        "ay": ay,
        "ax": ax,
        "axt": ax.transpose(0, 2, 1),
        "ayt": ay.transpose(0, 2, 1),
        "rep": rep[None],
        "fold": fold[None],
        "eye": eye4[None],
    }
    places, packed, start = {}, [], 0
    pack_cols = max(v.shape[2] for v in pieces.values())
    for k, v in pieces.items():
        assert v.shape[1] % 16 == 0
        places[k] = (start, v.shape)
        start += v.shape[0] * v.shape[1]
        flat_rows = v.reshape(-1, v.shape[2])
        packed.append(np.pad(flat_rows, ((0, 0), (0, pack_cols - v.shape[2]))))
    tables = {
        "kz_all": kz_all,
        "pack": const(np.concatenate(packed)),
        "sum_o": const(sum_o),
    }
    rows = cx * cy
    brow = qy * cx
    n_a = ny * nx

    def call(first, ins):
        args = dict(ins, **tables)
        t = 1 if first else 3
        outs = {
            "down": jax.ShapeDtypeStruct((rows, lanes), bf16 if first else f32),
            "hat": jax.ShapeDtypeStruct((t, modes, 2 * chan), f32),
        }
        if first:
            outs["pt"] = jax.ShapeDtypeStruct((chan, 2 * chan), f32)
        scratch = {
            "y": pltpu.VMEM((t, MY * cx, MZ * chan), f32),
            "land_a": pltpu.VMEM((t, 2, n_a, brow, blane // 2), f32),
            "p": pltpu.VMEM((t, 2, nz, mrow, blane // 2), f32),
            "land_b": pltpu.VMEM((t, 2, nz, mrow, blane // 2), f32),
            "c": pltpu.VMEM((2, nz, mrow, blane // 2), f32),
            "cat": pltpu.VMEM((nz * mrow, blane // 2), f32),
            "v": pltpu.VMEM((MY * cx, MZ * chan), f32),
            "v2": pltpu.VMEM((rows, MZ * chan), bf16),
            "kz": pltpu.VMEM((lanes, MZ * chan), bf16),
            "kz_sem": pltpu.SemaphoreType.DMA((2 * nx,)),
            "p4": pltpu.VMEM((256, 256), bf16),
        }
        sems = {"c": nz, "d": n_a}
        for k in range(t):
            sems["a%d" % k] = n_a
            sems["b%d" % k] = nz
        if first:
            scratch["pt_a"] = pltpu.VMEM((n_a, chan, 2 * chan), f32)
            scratch["pt_b"] = pltpu.VMEM((nz, chan, 2 * chan), f32)
            sems["pa"] = n_a
            sems["pb"] = nz
        for k, n in sems.items():
            scratch[k + "_s"] = pltpu.SemaphoreType.DMA((2, n))
            scratch[k + "_r"] = pltpu.SemaphoreType.DMA((2, n))
        cfg = dict(
            places=places,
            nz=nz, ny=ny, nx=nx, first=first, brow=brow, blane=blane, mrow=mrow,
            scales=(a_scale, b_scale), chan=chan,
            names=list(args) + list(outs) + list(scratch),
        )
        vmem = pl.BlockSpec(memory_space=pltpu.VMEM)
        got = pl.pallas_call(
            functools.partial(layer_kernel, cfg),
            out_shape=list(outs.values()),
            in_specs=[
                pl.BlockSpec(memory_space=pltpu.HBM) if k == "kz_all" else vmem
                for k in args
            ],
            out_specs=[vmem] * len(outs),
            scratch_shapes=list(scratch.values()),
            compiler_params=pltpu.CompilerParams(
                collective_id=1 if first else 0,
                has_side_effects=True,
                vmem_limit_bytes=48 * 1024 * 1024,
            ),
            name="layer_one" if first else "layer_two",
        )(*args.values())
        return dict(zip(outs, got))

    flat = (rows, lanes)
    gin = grid_input.reshape(flat)
    value_one, slope_one = gelu_both(pre_one.reshape(flat).astype(f32))
    _, slope_two = gelu_both(pre_two.reshape(flat).astype(f32))
    mid = value_one.astype(bf16)
    dz_two = (grad_output.reshape(flat).astype(f32) * slope_two).astype(bf16)
    two = call(
        False,
        {
            "dz": dz_two,
            "mid": mid,
            "gin": gin,
            "weights": spectral_two.reshape(modes, chan * chan),
            "point": point_two,
        },
    )
    dz_one = (two["down"] * slope_one).astype(bf16)
    one = call(
        True,
        {
            "dz": dz_one,
            "mid": mid,
            "gin": gin,
            "dz_two": dz_two,
            "weights": spectral_one.reshape(modes, chan * chan),
            "point": point_one,
        },
    )
    step = 1024
    small = [pl.BlockSpec((t, modes, 2 * chan), lambda n: (0, 0, 0)) for t in (1, 3)]
    large = pl.BlockSpec((modes, step), lambda n: (0, n))
    spec_one, spec_two = pl.pallas_call(
        functools.partial(outer_kernel, chan),
        grid=(chan * chan // step,),
        out_shape=[jax.ShapeDtypeStruct((modes, chan * chan), f32)] * 2,
        in_specs=small + [pl.BlockSpec((step, chan), lambda n: (n, 0))],
        out_specs=[large] * 2,
        name="outer",
    )(one["hat"], two["hat"], tables["sum_o"])
    return (
        one["down"].reshape(grid_input.shape),
        spec_one.reshape(spectral_one.shape),
        spec_two.reshape(spectral_two.shape),
        one["pt"][:, chan:],
        one["pt"][:, :chan],
    )


def solution(mesh):
    grid = P("gz", "gy", "gx")
    spec = P("gz", "gy", "gx", None)
    return jax.shard_map(
        on_device,
        mesh=mesh,
        in_specs=(grid, grid, grid, grid, spec, spec, P(), P()),
        out_specs=(grid, spec, spec, P(), P()),
        check_vma=False,
    )
```
